256 devices in a mesh: expert: 8 (over z_hi, core), cuts: 32 (over y, z_lo, x).
Axes of the slice: x: 4, y: 4, z: 8 (z_hi: 4, z_lo: 2; z = z_hi * 2 + z_lo), core: 2. Of those that a mesh axis runs over, the one named last changes fastest.
Arguments:
- out_grad: bfloat16 [2048, 3072], P(('expert', 'cuts')), may hold values from -6 to 6
- routes: int32 [2048, 2], P(('expert', 'cuts')), may hold values from 0 to 7, all different within a row; in each aligned block of 8 rows (0 to 7, 8 to 15, ...) at most 4 rows name the same one
- gate_weight: float32 [2048, 2], P(('expert', 'cuts')), may hold values from 0.1 to 1
- gate_proj: bfloat16 [8, 3072, 16384], P('expert', None, 'cuts'), may hold values from -0.109375 to 0.109375
- up_proj: bfloat16 [8, 3072, 16384], P('expert', None, 'cuts'), may hold values from -0.109375 to 0.109375
- down_proj: bfloat16 [8, 16384, 3072], P('expert', 'cuts'), may hold values from -0.046875 to 0.046875
- saved_gate: bfloat16 [8, 1024, 16384], P('expert', None, 'cuts'), may hold values from -6 to 6
- saved_up: bfloat16 [8, 1024, 16384], P('expert', None, 'cuts'), may hold values from -6 to 6
Outputs:
- input_grad: bfloat16 [2048, 3072], P(('expert', 'cuts'))
The draws below stay inside these ranges and needn't reach their ends.
Inputs may be any that keep to these rules, and one draw needn't show every extreme that they name: `routes`: each token names two different experts. Among the 8 tokens of one device no expert is named more than 4 times, and in some devices one expert is named exactly 4 times.
All inputs are finite; a program needn't handle non-finite values.
Results may differ from the reference program's by a relative error of at most 0.0057.
Values may be sent and summed in bfloat16 or wider, within the bound.
No kernel may reach another device: no remote copies, remote signals or barrier semaphores. Data moves between devices by JAX's collectives and lax.ppermute only.
A program may use at most 128 MiB of HBM per device.

```python
import math
import jax
import jax.numpy as jnp
import numpy as np
from jax import lax

D = 3072
FF = 16384
TOK_DEV = 8
EXPERTS = 8
CAP = 4
ROWS = 1024
TOKENS = 2048
N_EXPERT = 8
N_CUTS = 32


def level_of(own_key, shape, pieces, smallest, top_value):
    level, own = 1.0, jax.random.fold_in(own_key, 6)
    for dim, parts in pieces:
        steps = jnp.exp(jax.random.uniform(jax.random.fold_in(own, dim), (parts,), jnp.float32, smallest / len(pieces), top_value / len(pieces)))
        level = level * jnp.repeat(steps, shape[dim] // parts).reshape([-1 if axis == dim else 1 for axis in range(len(shape))])
    return level


def deal_out(stream_key, own, number, rows, number_of, top, most, lean):
    sequence = jax.random.permutation(stream_key, number_of)
    crowded, usual = load_shares(number_of, rows * top, most, lean, True), load_shares(number_of, rows * top, most, lean, False)
    places = jnp.arange(number_of)

    def named(tallies, offset_by):
        used = int((tallies > 0).sum())
        fixed = max(1, used // 4)
        passed = fixed + (places - fixed + offset_by * (used - fixed)) % max(1, number_of - fixed)
        return jnp.zeros((number_of,), jnp.int32).at[sequence[jnp.where(places < fixed, places, passed)]].set(jnp.asarray(tallies, jnp.int32))

    tallies = jnp.where(number % 4 == 0, named(crowded, number // 4), named(usual, number - number // 4 - 1))
    mixed = jax.random.permutation(jax.random.fold_in(own, 3), number_of)
    giver, taker = mixed[0:number_of // 2 * 2:2], mixed[1:number_of // 2 * 2:2]
    slack = jnp.minimum(tallies[giver] - 1, most - tallies[taker]) // 2
    slack = jnp.where((giver == sequence[0]) | (taker == sequence[0]) | (tallies[taker] == 0), 0, jnp.maximum(slack, 0))
    passed = jax.random.randint(jax.random.fold_in(own, 4), (number_of // 2,), 0, 1 << 20) % (slack + 1)
    tallies = tallies.at[giver].add(-passed).at[taker].add(passed)
    labels = jnp.searchsorted(jnp.cumsum(tallies), jnp.arange(rows * top), side="right").astype(jnp.int32)
    grid = labels.reshape(top, rows).T
    grid = grid[jax.random.permutation(jax.random.fold_in(own, 1), rows)]
    offset_by = jax.random.randint(jax.random.fold_in(own, 2), (rows, 1), 0, top)
    return jnp.take_along_axis(grid, (jnp.arange(top)[None, :] + offset_by) % top, axis=1)


def load_shares(number_of, total, most, slope, full):
    weights = [(1 << 20) // math.isqrt(grade ** slope) + 1 for grade in range(1, number_of + 1)]
    largest = most if full else min(most, max(-(-total // number_of), total * weights[0] // sum(weights)))
    least = 1 if total - largest >= number_of - 1 else 0
    counts, spare = [largest] + [least] * (number_of - 1), total - largest - least * (number_of - 1)
    while spare > 0:
        free = [i for i in range(1, number_of) if counts[i] < largest] or [i for i in range(1, number_of) if counts[i] < most]
        pool, left = sum([weights[i] for i in free]), spare
        for i in free:
            addition = min(most - counts[i], max(1, left * weights[i] // pool), spare)
            counts[i] = counts[i] + addition
            spare = spare - addition
    return np.array(counts)


def bell_draw(key, dims, deviation, limit, split=(), kind=jnp.bfloat16):
    entries = deviation * jax.random.normal(key, dims, jnp.float32)
    if split:
        entries = entries * level_of(key, dims, split, -0.22, 0.18)
    return jnp.clip(entries, -limit, limit).astype(kind)


def setup_inputs(seed: int = 0) -> dict:
    key_list = jax.random.split(jax.random.key(seed), 9)
    out_grad = bell_draw(key_list[0], (TOKENS, D), 1.0, 6.0, ((0, 256),))
    routes_keys = jax.random.split(jax.random.fold_in(key_list[1], 1), TOKENS // TOK_DEV)
    routes_turns = jax.random.permutation(jax.random.fold_in(key_list[1], 3), TOKENS // TOK_DEV)
    routes = jax.vmap(lambda own, number: deal_out(jax.random.fold_in(key_list[1], 2), own, number, TOK_DEV, EXPERTS, 2, CAP, 2))(routes_keys, routes_turns).reshape((TOKENS, 2))
    gate_weight = jnp.clip(0.1 + 0.9 * jax.random.uniform(key_list[2], (TOKENS, 2), jnp.float32) ** level_of(key_list[2], (TOKENS, 2), ((0, 256),), -0.2, 0.2), 0.1, 1.0)
    gate_proj = bell_draw(key_list[3], (EXPERTS, D, FF), D ** -0.5, 0.109375, ((0, 8), (2, 32)))
    up_proj = bell_draw(key_list[4], (EXPERTS, D, FF), D ** -0.5, 0.109375, ((0, 8), (2, 32)))
    down_proj = bell_draw(key_list[5], (EXPERTS, FF, D), FF ** -0.5, 0.046875, ((0, 8), (1, 32)))
    saved_gate = bell_draw(key_list[6], (EXPERTS, ROWS, FF), 1.0, 6.0, ((0, 8), (2, 32)))
    saved_up = bell_draw(key_list[7], (EXPERTS, ROWS, FF), 1.0, 6.0, ((0, 8), (2, 32)))
    return dict(out_grad=out_grad, routes=routes, gate_weight=gate_weight, gate_proj=gate_proj, up_proj=up_proj, down_proj=down_proj, saved_gate=saved_gate, saved_up=saved_up)


def rank_slots(flat_routes):
    count = flat_routes.shape[-1]
    positions = jnp.arange(count, dtype=jnp.int32)
    before = positions[:, None] < positions[None, :]
    matches = flat_routes[..., :, None] == flat_routes[..., None, :]
    return jnp.sum(jnp.logical_and(matches, before), axis=-2).astype(jnp.int32)


def expert_rows(grad_rows, gate_mat, up_mat, down_mat, pre_gate, pre_up):
    contract = (((1,), (1,)), ((), ()))
    hidden_grad = lax.dot_general(grad_rows, down_mat, contract, preferred_element_type=jnp.float32)
    gate_vals = pre_gate.astype(jnp.float32)
    up_vals = pre_up.astype(jnp.float32)
    sigmoid_gate = jax.nn.sigmoid(gate_vals)
    up_grad = (hidden_grad * gate_vals * sigmoid_gate).astype(jnp.bfloat16)
    gate_grad = (hidden_grad * up_vals * sigmoid_gate * (1.0 + gate_vals * (1.0 - sigmoid_gate))).astype(jnp.bfloat16)
    partial_value = lax.dot_general(gate_grad, gate_mat, contract, preferred_element_type=jnp.float32)
    return partial_value + lax.dot_general(up_grad, up_mat, contract, preferred_element_type=jnp.float32)


def reference(out_grad, routes, gate_weight, gate_proj, up_proj, down_proj, saved_gate, saved_up):
    device_count = N_EXPERT * N_CUTS
    block_routes = routes.reshape(device_count, 2 * TOK_DEV)
    slot_index = rank_slots(block_routes)
    device_ids = jnp.arange(device_count, dtype=jnp.int32)
    source_expert = device_ids // N_CUTS
    source_cut = device_ids % N_CUTS
    row_index = (source_cut * N_EXPERT + source_expert)[:, None] * CAP + slot_index
    routed = (gate_weight[:, :, None] * out_grad.astype(jnp.float32)[:, None, :]).astype(jnp.bfloat16)
    routed = routed.reshape(TOKENS * 2, D)
    expert_flat = routes.reshape(-1).astype(jnp.int32)
    row_flat = row_index.reshape(-1).astype(jnp.int32)
    expert_grad = jnp.zeros((EXPERTS, ROWS, D), jnp.bfloat16).at[expert_flat, row_flat].set(routed)
    partial_value = lax.map(lambda items: expert_rows(*items), (expert_grad, gate_proj, up_proj, down_proj, saved_gate, saved_up))
    picked = partial_value[expert_flat, row_flat].reshape(TOKENS, 2, D)
    return jnp.sum(picked, axis=1).astype(jnp.bfloat16)
```

```python
import jax
import jax.numpy as jnp
from jax import lax
from jax.sharding import Mesh, PartitionSpec as P

BF = jnp.bfloat16
F32 = jnp.float32
Z = ("zh", "core", "zl")


def hop(value, axis, step):
    count = lax.axis_size(axis)
    return lax.ppermute(value, axis, [(i, (i + step) % count) for i in range(count)])


def rank_slots(flat_routes):
    count = flat_routes.shape[-1]
    positions = jnp.arange(count, dtype=jnp.int32)
    before = positions[:, None] < positions[None, :]
    matches = flat_routes[:, None] == flat_routes[None, :]
    return jnp.sum(jnp.logical_and(matches, before), axis=-2)


def expert_rows(grad_rows, gate_mat, up_mat, down_mat, pre_gate, pre_up):
    contract = (((1,), (1,)), ((), ()))
    hidden_grad = lax.dot_general(grad_rows, down_mat, contract, preferred_element_type=F32)
    gate_vals = pre_gate.astype(F32)
    up_vals = pre_up.astype(F32)
    sigmoid_gate = jax.nn.sigmoid(gate_vals)
    up_grad = (hidden_grad * gate_vals * sigmoid_gate).astype(BF)
    gate_grad = (
        hidden_grad * up_vals * sigmoid_gate * (1.0 + gate_vals * (1.0 - sigmoid_gate))
    ).astype(BF)
    partial_value = lax.dot_general(gate_grad, gate_mat, contract, preferred_element_type=F32)
    return partial_value + lax.dot_general(up_grad, up_mat, contract, preferred_element_type=F32)


def rolled(value, axis, start):
    size = value.shape[axis]
    return lax.dynamic_slice_in_dim(jnp.concatenate([value, value], axis), start, size, axis)


def shards(out_grad, routes, gate_weight, gate_proj, up_proj, down_proj, saved_gate, saved_up):
    tok, dim = out_grad.shape
    hidden = saved_gate.shape[2]
    my_x, my_y = lax.axis_index("x"), lax.axis_index("y")
    flat_routes = routes.reshape(-1)
    own_spots = flat_routes * 4 + rank_slots(flat_routes)
    routed = (gate_weight[:, :, None] * out_grad.astype(F32)[:, None, :]).astype(BF)
    routed = routed.reshape(2 * tok, dim)
    places = jnp.arange(64, dtype=jnp.int32)
    spot_of = (places // 8) * 4 + places % 4
    placing = (spot_of[:, None] == own_spots[None, :]).astype(BF)
    outgoing = jnp.dot(placing, routed, preferred_element_type=F32).astype(BF)
    arrived = lax.all_to_all(outgoing.reshape(16, 4, dim), Z, split_axis=0, concat_axis=0, tiled=True)
    arrived = arrived.reshape(2, 4, 2, 4, dim).transpose(0, 2, 1, 3, 4).reshape(2, 32, dim)

    def saved(value, first, second):
        blocks = value[0].reshape(4, 2, 4, 2, 16, hidden)
        blocks = rolled(rolled(blocks, 0, my_y), 2, my_x)
        one = blocks[:, :, :, 0].transpose(0, 2, 1, 3, 4).reshape(4, 128, hidden)
        two = blocks[:, :, :, 1].transpose(2, 0, 1, 3, 4).reshape(4, 128, hidden)
        return one, two

    gates = saved(saved_gate, 0, 1)
    ups = saved(saved_up, 0, 1)

    def spread(value, axis):
        return [value] + [hop(value, axis, -r) for r in (1, 2, 3)]

    first = [jnp.concatenate(spread(arrived[h], a), 0) for h, a in ((0, "x"), (1, "y"))]
    second = [spread(first[h], a) for h, a in ((0, "y"), (1, "x"))]

    parts = {}
    for group in ((0,), (1, 3), (2,)):
        rows = jnp.concatenate([second[h][r] for r in group for h in (0, 1)], 0)
        pre_gate = jnp.concatenate([gates[h][r] for r in group for h in (0, 1)], 0)
        pre_up = jnp.concatenate([ups[h][r] for r in group for h in (0, 1)], 0)
        out = expert_rows(rows, gate_proj[0], up_proj[0], down_proj[0], pre_gate, pre_up)
        for i, (r, h) in enumerate([(r, h) for r in group for h in (0, 1)]):
            parts[h, r] = out[i * 128:(i + 1) * 128]

    def collect(pieces, axis):
        total = pieces[0]
        got = [hop(pieces[r].astype(BF), axis, r) for r in (1, 2, 3)]
        for value in got:
            total = total + value.astype(F32)
        return total

    big = [collect([parts[h, r] for r in range(4)], a) for h, a in ((0, "y"), (1, "x"))]
    small = [
        collect([big[h][r * 32:(r + 1) * 32] for r in range(4)], a) for h, a in ((0, "x"), (1, "y"))
    ]
    back = jnp.stack(small).astype(BF).reshape(2, 2, 4, 4, dim).transpose(0, 2, 1, 3, 4)
    returned = lax.all_to_all(back.reshape(16, 4, dim), Z, split_axis=0, concat_axis=0, tiled=True)
    picking = jnp.sum(
        (spot_of[None, None, :] == own_spots.reshape(tok, 2, 1)).astype(BF), axis=1
    )
    summed = jnp.dot(picking, returned.reshape(64, dim), preferred_element_type=F32)
    return summed.astype(BF)


def solution(mesh):
    fine = Mesh(mesh.devices.reshape(4, 2, 4, 2, 4), ("zh", "core", "y", "zl", "x"))
    expert, cuts = ("zh", "core"), ("y", "zl", "x")
    rows = P(expert + cuts, None)
    in_specs = (
        rows,
        rows,
        rows,
        P(expert, None, cuts),
        P(expert, None, cuts),
        P(expert, cuts, None),
        P(expert, None, cuts),
        P(expert, None, cuts),
    )
    return jax.shard_map(shards, mesh=fine, in_specs=in_specs, out_specs=rows, check_vma=False)
```

```python
import jax
import jax.numpy as jnp
from jax import lax
from jax.sharding import Mesh, PartitionSpec as P

BF = jnp.bfloat16
F32 = jnp.float32
Z = ("zh", "zl")
SLAB = ("core", "y", "x")
SIDE = 4


def hop(value, order, step):
    pairs = []
    for core in range(2):
        for y in range(SIDE):
            for x in range(SIDE):
                to_y, to_x = (y, (x + step) % SIDE) if core == order else ((y + step) % SIDE, x)
                pairs.append(((core * SIDE + y) * SIDE + x, (core * SIDE + to_y) * SIDE + to_x))
    return lax.ppermute(value, SLAB, pairs)


def swap(value):
    return lax.ppermute(value, "core", [(0, 1), (1, 0)])


def rank_slots(flat_routes):
    count = flat_routes.shape[0]
    positions = jnp.arange(count, dtype=jnp.int32)
    before = positions[:, None] < positions[None, :]
    matches = flat_routes[:, None] == flat_routes[None, :]
    return jnp.sum(jnp.logical_and(matches, before), axis=0)


def exact(choice, value):
    return jnp.dot(choice.astype(BF), value, preferred_element_type=F32)


def expert_rows(grad_rows, gate_mat, up_mat, down_mat, pre_gate, pre_up):
    contract = (((1,), (1,)), ((), ()))
    hidden_grad = lax.dot_general(grad_rows, down_mat, contract, preferred_element_type=F32)
    gate_vals = pre_gate.astype(F32)
    up_vals = pre_up.astype(F32)
    sigmoid_gate = jax.nn.sigmoid(gate_vals)
    up_grad = (hidden_grad * gate_vals * sigmoid_gate).astype(BF)
    gate_grad = (
        hidden_grad * up_vals * sigmoid_gate * (1.0 + gate_vals * (1.0 - sigmoid_gate))
    ).astype(BF)
    partial_value = lax.dot_general(gate_grad, gate_mat, contract, preferred_element_type=F32)
    partial_value += lax.dot_general(up_grad, up_mat, contract, preferred_element_type=F32)
    return partial_value.astype(BF)


def shards(out_grad, routes, gate_weight, gate_proj, up_proj, down_proj, saved_gate, saved_up):
    tok, dim = out_grad.shape
    my_x, my_y = lax.axis_index("x"), lax.axis_index("y")
    core = lax.axis_index("core")

    flat_routes = routes.reshape(-1)
    slot = rank_slots(flat_routes)
    key = ((flat_routes // 2) * 2 + (flat_routes + core) % 2) * 4 + slot
    key = key.reshape(tok, 2)
    places = jnp.arange(64, dtype=jnp.int32)
    place_key = ((places // 16) * 2 + (places // 4) % 2) * 4 + places % 4
    match = place_key[:, None, None] == key[None, :, :]
    weight = jnp.sum(jnp.where(match, gate_weight[None], 0.0), axis=(1, 2))
    chosen = jnp.any(match, axis=2)
    outgoing = (exact(chosen, out_grad) * weight[:, None]).astype(BF)
    arrived = lax.all_to_all(outgoing, Z, split_axis=0, concat_axis=0, tiled=True)
    turned = (places % 32) // 4 * 8 + places // 32 * 4 + places % 4
    turn = turned[:, None] == places[None, :]
    own = exact(turn, arrived).astype(BF)

    def saved_rows(group):
        count = len(group) * 256
        i = jnp.arange(count, dtype=jnp.int32)
        outer = jnp.asarray(group, jnp.int32)[i // 256]
        source = (core + (i // 128) % 2) % 2
        inner = jnp.asarray((0, 3, 1, 2), jnp.int32)[(i // 32) % 4]
        step_y = jnp.where(source == 0, outer, inner)
        step_x = jnp.where(source == 0, inner, outer)
        z = (i // 4) % 8
        block = ((my_y + step_y) % 4 * 2 + z % 2) * 4 + (my_x + step_x) % 4
        row = block * 32 + ((z // 2) * 2 + source) * 4 + i % 4
        choice = row[:, None] == jnp.arange(saved_gate.shape[1], dtype=jnp.int32)[None, :]
        return exact(choice, saved_gate[0]).astype(BF), exact(choice, saved_up[0]).astype(BF)

    pre = (saved_rows((3, 1)), saved_rows((2,)), saved_rows((0,)))
    own, pre = lax.optimization_barrier((own, pre))
    pre_sides, pre_end, pre_line = pre

    before, after = hop(own, 0, 1), hop(own, 0, -1)
    far = hop(before, 0, 1)
    ring = (own, before, after, far)
    line = [jnp.concatenate([v[k * 32:k * 32 + 32] for v in ring], 0) for k in (0, 1)]
    weights = (gate_proj[0], up_proj[0], down_proj[0])
    line_other = swap(line[1])
    back0, ahead1 = hop(line[0], 1, 1), hop(line[1], 1, -1)
    line, line_other = lax.optimization_barrier((line, line_other))
    back1, ahead0 = hop(line[1], 1, 1), hop(line[0], 1, -1)
    end0, end1 = hop(back0, 1, 1), hop(ahead1, 1, -1)
    ahead_other, back_other = swap(ahead1), swap(back1)
    end_other = swap(end1)
    middle = expert_rows(jnp.concatenate([line[0], line_other], 0), *weights, *pre_line)
    middle, back_other, ahead0 = lax.optimization_barrier((middle, back_other, ahead0))
    sides = expert_rows(
        jnp.concatenate([back0, back_other, ahead0, ahead_other], 0), *weights, *pre_sides
    )
    to_back0, to_back1, to_ahead0, to_ahead1 = [sides[k * 128:k * 128 + 128] for k in range(4)]
    to_back1, to_ahead1 = swap(to_back1), swap(to_ahead1)
    got_ahead1, got_back0 = hop(to_back1, 1, -1), hop(to_ahead0, 1, 1)
    sides, end0, end_other = lax.optimization_barrier((sides, end0, end_other))
    ends = expert_rows(jnp.concatenate([end0, end_other], 0), *weights, *pre_end)
    far0, far1 = hop(ends[:128], 1, -1), hop(swap(ends[128:]), 1, 1)
    middle0, middle1 = middle[:128], swap(middle[128:])
    got_ahead0 = hop((to_back0.astype(F32) + far0.astype(F32)).astype(BF), 1, -1)
    got_back1 = hop((to_ahead1.astype(F32) + far1.astype(F32)).astype(BF), 1, 1)

    def add(*values):
        return sum(v.astype(F32) for v in values)

    sums = [add(middle0, got_back0, got_ahead0), add(middle1, got_back1, got_ahead1)]
    mine, to_before, to_after, to_far = [
        jnp.concatenate([s[k * 32:k * 32 + 32] for s in sums], 0) for k in range(4)
    ]
    passed = hop(to_far.astype(BF), 0, -1)
    got_before = hop(to_after.astype(BF), 0, 1)
    got_after = hop(add(to_before, passed).astype(BF), 0, -1)
    total = add(mine, got_before, got_after).astype(BF)
    turn_back = turned[None, :] == places[:, None]
    total = exact(turn_back, total).astype(BF)
    returned = lax.all_to_all(total, Z, split_axis=0, concat_axis=0, tiled=True)
    return exact(chosen.T, returned).astype(BF)


def solution(mesh):
    fine = Mesh(mesh.devices.reshape(4, 2, 4, 2, 4), ("zh", "core", "y", "zl", "x"))
    expert, cuts = ("zh", "core"), ("y", "zl", "x")
    rows = P(expert + cuts, None)
    in_specs = (
        rows,
        rows,
        rows,
        P(expert, None, cuts),
        P(expert, None, cuts),
        P(expert, cuts, None),
        P(expert, None, cuts),
        P(expert, None, cuts),
    )
    return jax.shard_map(shards, mesh=fine, in_specs=in_specs, out_specs=rows, check_vma=False)
```

```python
import jax
import jax.numpy as jnp
from jax import lax
from jax.sharding import Mesh, PartitionSpec as P

BF = jnp.bfloat16
F32 = jnp.float32
SLAB = ("core", "y", "x")
SIDE = 4


def hop(value, order, step, leave=False, join=False):
    pairs = []
    for core in range(2):
        axis_core = 1 - core if join else core
        to_core = 1 - core if leave or join else core
        for y in range(SIDE):
            for x in range(SIDE):
                to_y, to_x = y, x
                if axis_core == order:
                    to_x = (x + step) % SIDE
                else:
                    to_y = (y + step) % SIDE
                pairs.append(((core * SIDE + y) * SIDE + x, (to_core * SIDE + to_y) * SIDE + to_x))
    return lax.ppermute(value, SLAB, pairs)


def swap(value):
    return lax.ppermute(value, "core", [(0, 1), (1, 0)])


def rank_slots(flat_routes):
    count = flat_routes.shape[0]
    positions = jnp.arange(count, dtype=jnp.int32)
    before = positions[:, None] < positions[None, :]
    matches = flat_routes[:, None] == flat_routes[None, :]
    return jnp.sum(jnp.logical_and(matches, before), axis=0)


def exact(choice, value):
    return jnp.dot(choice.astype(BF), value, preferred_element_type=F32)


def expert_rows(grad_rows, gate_mat, up_mat, down_mat, pre_gate, pre_up):
    contract = (((1,), (1,)), ((), ()))
    hidden_grad = lax.dot_general(grad_rows, down_mat, contract, preferred_element_type=F32)
    gate_vals = pre_gate.astype(F32)
    up_vals = pre_up.astype(F32)
    sigmoid_gate = jax.nn.sigmoid(gate_vals)
    up_grad = (hidden_grad * gate_vals * sigmoid_gate).astype(BF)
    gate_grad = (
        hidden_grad * up_vals * sigmoid_gate * (1.0 + gate_vals * (1.0 - sigmoid_gate))
    ).astype(BF)
    partial_value = lax.dot_general(gate_grad, gate_mat, contract, preferred_element_type=F32)
    partial_value += lax.dot_general(up_grad, up_mat, contract, preferred_element_type=F32)
    return partial_value.astype(BF)


def add(*values):
    return sum(v.astype(F32) for v in values)


def shards(out_grad, routes, gate_weight, gate_proj, up_proj, down_proj, saved_gate, saved_up):
    tok, dim = out_grad.shape
    my_x, my_y = lax.axis_index("x"), lax.axis_index("y")
    core = lax.axis_index("core")

    flat_routes = routes.reshape(-1)
    slot = rank_slots(flat_routes)
    key = ((flat_routes // 2) * 2 + (flat_routes + core) % 2) * 4 + slot
    key = key.reshape(tok, 2)
    places = jnp.arange(32, dtype=jnp.int32)
    far_z = ((places // 8 + lax.axis_index("zh")) % 4) * 2 + (places // 4) % 2
    match = (far_z * 4 + places % 4)[:, None, None] == key[None, :, :]
    weight = jnp.sum(jnp.where(match, gate_weight[None], 0.0), axis=(1, 2))
    chosen = jnp.any(match, axis=2)
    outgoing = (exact(chosen, out_grad) * weight[:, None]).astype(BF)
    arrived = [outgoing[:8]] + [
        lax.ppermute(outgoing[8 * k:8 * k + 8], "zh", [(i, (i + k) % 4) for i in range(4)])
        for k in (1, 2, 3)
    ]
    arrived = jnp.concatenate(arrived, 0)
    pair = [(0, 1), (1, 0)]
    arrived = jnp.concatenate([arrived, lax.ppermute(arrived, "zl", pair)], 0)
    places = jnp.arange(64, dtype=jnp.int32)
    turned = (places % 32) // 4 * 8 + places // 32 * 4 + places % 4
    turn = turned[:, None] == places[None, :]
    own = exact(turn, arrived).astype(BF)
    own, saved_gate, saved_up = lax.optimization_barrier((own, saved_gate, saved_up))

    def saved_rows(*parts):
        i = jnp.arange(128 * len(parts), dtype=jnp.int32)
        outer = jnp.asarray([p[0] for p in parts], jnp.int32)[i // 128]
        source = (core + jnp.asarray([p[1] for p in parts], jnp.int32)[i // 128]) % 2
        inner = jnp.asarray((0, 3, 1, 2), jnp.int32)[(i // 32) % 4]
        step_y = jnp.where(source == 0, outer, inner)
        step_x = jnp.where(source == 0, inner, outer)
        low = (lax.axis_index("zl") + (i // 16) % 2) % 2
        high = (lax.axis_index("zh") + 4 - (i // 4) % 4) % 4
        block = ((my_y + step_y) % 4 * 2 + low) * 4 + (my_x + step_x) % 4
        row = block * 32 + (high * 2 + source) * 4 + i % 4
        choice = row[:, None] == jnp.arange(saved_gate.shape[1], dtype=jnp.int32)[None, :]
        return exact(choice, saved_gate[0]).astype(BF), exact(choice, saved_up[0]).astype(BF)

    pre = (
        saved_rows((0, 0), (0, 1)),
        saved_rows((3, 0), (1, 1)),
        saved_rows((1, 0), (3, 1)),
        saved_rows((2, 0), (2, 1)),
    )
    far = hop(own, 0, 2)
    before, after = hop(own, 0, 1), hop(own, 0, -1)
    (before, after, far), pre = lax.optimization_barrier(((before, after, far), pre))
    pre_line, pre_early, pre_late, pre_end = pre
    ring = (own, before, after, far)
    line = [jnp.concatenate([v[k * 32:k * 32 + 32] for v in ring], 0) for k in (0, 1)]
    weights = (gate_proj[0], up_proj[0], down_proj[0])

    def work(mine, others, saved):
        result = expert_rows(jnp.concatenate([mine, others], 0), *weights, *saved)
        return result[:128], result[128:]

    line_other = swap(line[1])
    back0, ahead1 = hop(line[0], 1, 1), hop(line[1], 1, -1)
    line, line_other = lax.optimization_barrier((line, line_other))
    back_other, ahead0 = hop(line[1], 1, 1, leave=True), hop(line[0], 1, -1)
    end0, end1 = hop(back0, 1, 1), hop(ahead1, 1, -1, leave=True)
    ahead_other = swap(ahead1)
    middle = work(line[0], line_other, pre_line)
    middle, ahead_other = lax.optimization_barrier((middle, ahead_other))
    early = work(back0, ahead_other, pre_early)
    early, ahead0, back_other = lax.optimization_barrier((early, ahead0, back_other))
    got_ahead0, got_back1 = hop(early[0], 1, -1), hop(early[1], 1, 1, join=True)
    late = work(ahead0, back_other, pre_late)
    middle_other = swap(middle[1])
    late, end0, end1, middle_other = lax.optimization_barrier((late, end0, end1, middle_other))
    ends = work(end0, end1, pre_end)
    far0, far1 = hop(ends[0], 1, 1), hop(ends[1], 1, -1, join=True)
    late_other = swap(late[1])
    far0, far1, got_ahead0, got_back1, late_other = lax.optimization_barrier(
        (far0, far1, got_ahead0, got_back1, late_other)
    )
    got_back0 = hop(add(late[0], far0).astype(BF), 1, 1)
    got_ahead1 = hop(add(late_other, far1).astype(BF), 1, -1)
    sums = [add(middle[0], got_back0, got_ahead0), add(middle_other, got_back1, got_ahead1)]
    mine, to_before, to_after, to_far = [
        jnp.concatenate([s[k * 32:k * 32 + 32] for s in sums], 0) for k in range(4)
    ]
    got_far = hop(to_far.astype(BF), 0, 2)
    got_before = hop(to_after.astype(BF), 0, 1)
    got_after = hop(to_before.astype(BF), 0, -1)
    total = add(mine, got_before, got_after, got_far)
    near_z = jnp.concatenate([total[:16], total[32:48]], 0)
    away_z = jnp.concatenate([total[16:32], total[48:]], 0).astype(BF)
    total = add(near_z, lax.ppermute(away_z, "zl", pair)).astype(BF)
    places = jnp.arange(32, dtype=jnp.int32)
    turn_back = (places // 4 % 2 * 16 + places // 8 * 4 + places % 4)[:, None] == places[None, :]
    total = exact(turn_back, total).astype(BF)
    returned = [total[:8]] + [
        lax.ppermute(total[8 * k:8 * k + 8], "zh", [(i, (i - k) % 4) for i in range(4)])
        for k in (1, 2, 3)
    ]
    return exact(chosen.T, jnp.concatenate(returned, 0)).astype(BF)


def solution(mesh):
    fine = Mesh(mesh.devices.reshape(4, 2, 4, 2, 4), ("zh", "core", "y", "zl", "x"))
    expert, cuts = ("zh", "core"), ("y", "zl", "x")
    rows = P(expert + cuts, None)
    in_specs = (
        rows,
        rows,
        rows,
        P(expert, None, cuts),
        P(expert, None, cuts),
        P(expert, cuts, None),
        P(expert, None, cuts),
        P(expert, None, cuts),
    )
    return jax.shard_map(shards, mesh=fine, in_specs=in_specs, out_specs=rows, check_vma=False)
```

```python
import jax
import jax.numpy as jnp
from jax import lax
from jax.sharding import Mesh, PartitionSpec as P

BF = jnp.bfloat16
F32 = jnp.float32
SLAB = ("core", "y", "x")
SIDE = 4


def hop(value, order, step, leave=False, join=False):
    pairs = []
    for core in range(2):
        axis_core = 1 - core if join else core
        to_core = 1 - core if leave or join else core
        for y in range(SIDE):
            for x in range(SIDE):
                to_y, to_x = y, x
                if axis_core == order:
                    to_x = (x + step) % SIDE
                else:
                    to_y = (y + step) % SIDE
                pairs.append(((core * SIDE + y) * SIDE + x, (to_core * SIDE + to_y) * SIDE + to_x))
    return lax.ppermute(value, SLAB, pairs)


def swap(value):
    return lax.ppermute(value, "core", [(0, 1), (1, 0)])


def rank_slots(flat_routes):
    count = flat_routes.shape[0]
    positions = jnp.arange(count, dtype=jnp.int32)
    before = positions[:, None] < positions[None, :]
    matches = flat_routes[:, None] == flat_routes[None, :]
    return jnp.sum(jnp.logical_and(matches, before), axis=0)


def exact(choice, value):
    return jnp.dot(choice.astype(BF), value, preferred_element_type=F32)


def expert_rows(grad_rows, gate_mat, up_mat, down_mat, pre_gate, pre_up):
    contract = (((1,), (1,)), ((), ()))
    hidden_grad = lax.dot_general(grad_rows, down_mat, contract, preferred_element_type=F32)
    gate_vals = pre_gate.astype(F32)
    up_vals = pre_up.astype(F32)
    sigmoid_gate = jax.nn.sigmoid(gate_vals)
    up_grad = (hidden_grad * gate_vals * sigmoid_gate).astype(BF)
    gate_grad = (
        hidden_grad * up_vals * sigmoid_gate * (1.0 + gate_vals * (1.0 - sigmoid_gate))
    ).astype(BF)
    partial_value = lax.dot_general(gate_grad, gate_mat, contract, preferred_element_type=F32)
    partial_value += lax.dot_general(up_grad, up_mat, contract, preferred_element_type=F32)
    return partial_value.astype(BF)


def add(*values):
    return sum(v.astype(F32) for v in values)


def shards(out_grad, routes, gate_weight, gate_proj, up_proj, down_proj, saved_gate, saved_up):
    tok, dim = out_grad.shape
    my_x, my_y = lax.axis_index("x"), lax.axis_index("y")
    core = lax.axis_index("core")

    flat_routes = routes.reshape(-1)
    slot = rank_slots(flat_routes)
    key = ((flat_routes // 2) * 2 + (flat_routes + core) % 2) * 4 + slot
    key = key.reshape(tok, 2)
    places = jnp.arange(32, dtype=jnp.int32)
    far_z = ((places // 8 + lax.axis_index("zh")) % 4) * 2 + (places // 4) % 2
    match = (far_z * 4 + places % 4)[:, None, None] == key[None, :, :]
    weight = jnp.sum(jnp.where(match, gate_weight[None], 0.0), axis=(1, 2))
    chosen = jnp.any(match, axis=2)
    outgoing = (exact(chosen, out_grad) * weight[:, None]).astype(BF)
    arrived = [outgoing[:8]] + [
        lax.ppermute(outgoing[8 * k:8 * k + 8], "zh", [(i, (i + k) % 4) for i in range(4)])
        for k in (1, 2, 3)
    ]
    arrived = jnp.concatenate(arrived, 0)
    pair = [(0, 1), (1, 0)]
    turned = (places % 16) // 4 * 8 + places // 16 * 4 + places % 4
    turn = turned[:, None] == places[None, :]
    own = exact(turn, arrived).astype(BF)
    layers = (own, lax.ppermute(own, "zl", pair))
    rings = [(v, hop(v, 0, 1), hop(v, 0, -1), hop(v, 0, 2)) for v in layers]
    line = [
        jnp.concatenate([v[k * 16:k * 16 + 16] for pieces in zip(*rings) for v in pieces], 0)
        for k in (0, 1)
    ]
    line, saved_gate, saved_up = lax.optimization_barrier((line, saved_gate, saved_up))

    def saved_rows(*parts):
        i = jnp.arange(128 * len(parts), dtype=jnp.int32)
        outer = jnp.asarray([p[0] for p in parts], jnp.int32)[i // 128]
        source = (core + jnp.asarray([p[1] for p in parts], jnp.int32)[i // 128]) % 2
        inner = jnp.asarray((0, 3, 1, 2), jnp.int32)[(i // 32) % 4]
        step_y = jnp.where(source == 0, outer, inner)
        step_x = jnp.where(source == 0, inner, outer)
        low = (lax.axis_index("zl") + (i // 16) % 2) % 2
        high = (lax.axis_index("zh") + 4 - (i // 4) % 4) % 4
        block = ((my_y + step_y) % 4 * 2 + low) * 4 + (my_x + step_x) % 4
        row = block * 32 + (high * 2 + source) * 4 + i % 4
        choice = row[:, None] == jnp.arange(saved_gate.shape[1], dtype=jnp.int32)[None, :]
        return exact(choice, saved_gate[0]).astype(BF), exact(choice, saved_up[0]).astype(BF)

    pre_line, pre_early, pre_late, pre_end = (
        saved_rows((0, 0), (0, 1)),
        saved_rows((3, 0), (1, 1)),
        saved_rows((1, 0), (3, 1)),
        saved_rows((2, 0), (2, 1)),
    )
    pre_line, pre_early, pre_late, pre_end = lax.optimization_barrier(
        (pre_line, pre_early, pre_late, pre_end)
    )
    weights = (gate_proj[0], up_proj[0], down_proj[0])

    def work(mine, others, saved):
        result = expert_rows(jnp.concatenate([mine, others], 0), *weights, *saved)
        return result[:128], result[128:]

    line_other = swap(line[1])
    back0, ahead1 = hop(line[0], 1, 1), hop(line[1], 1, -1)
    line, line_other = lax.optimization_barrier((line, line_other))
    back_other, ahead0 = hop(line[1], 1, 1, leave=True), hop(line[0], 1, -1)
    end0, end1 = hop(back0, 1, 1), hop(ahead1, 1, -1, leave=True)
    ahead_other = swap(ahead1)
    middle = work(line[0], line_other, pre_line)
    middle, ahead_other = lax.optimization_barrier((middle, ahead_other))
    early = work(back0, ahead_other, pre_early)
    early, ahead0, back_other = lax.optimization_barrier((early, ahead0, back_other))
    got_ahead0, got_back1 = hop(early[0], 1, -1), hop(early[1], 1, 1, join=True)
    late = work(ahead0, back_other, pre_late)
    middle_other = swap(middle[1])
    late, end0, end1, middle_other = lax.optimization_barrier((late, end0, end1, middle_other))
    ends = work(end0, end1, pre_end)
    far0, far1 = hop(ends[0], 1, 1), hop(ends[1], 1, -1, join=True)
    late_other = swap(late[1])
    far0, far1, got_ahead0, got_back1, late_other = lax.optimization_barrier(
        (far0, far1, got_ahead0, got_back1, late_other)
    )
    got_back0 = hop(add(late[0], far0).astype(BF), 1, 1)
    got_ahead1 = hop(add(late_other, far1).astype(BF), 1, -1)
    sums = [add(middle[0], got_back0, got_ahead0), add(middle_other, got_back1, got_ahead1)]
    mine, to_before, to_after, to_far = [
        jnp.concatenate([s[k * 32:k * 32 + 32] for s in sums], 0) for k in range(4)
    ]
    got_far = hop(to_far.astype(BF), 0, 2)
    got_before = hop(to_after.astype(BF), 0, 1)
    got_after = hop(to_before.astype(BF), 0, -1)
    total = add(mine, got_before, got_after, got_far)
    near_z = jnp.concatenate([total[:16], total[32:48]], 0)
    away_z = jnp.concatenate([total[16:32], total[48:]], 0).astype(BF)
    total = add(near_z, lax.ppermute(away_z, "zl", pair)).astype(BF)
    turn_back = turned[None, :] == places[:, None]
    total = exact(turn_back, total).astype(BF)
    returned = [total[:8]] + [
        lax.ppermute(total[8 * k:8 * k + 8], "zh", [(i, (i - k) % 4) for i in range(4)])
        for k in (1, 2, 3)
    ]
    return exact(chosen.T, jnp.concatenate(returned, 0)).astype(BF)


def solution(mesh):
    fine = Mesh(mesh.devices.reshape(4, 2, 4, 2, 4), ("zh", "core", "y", "zl", "x"))
    expert, cuts = ("zh", "core"), ("y", "zl", "x")
    rows = P(expert + cuts, None)
    in_specs = (
        rows,
        rows,
        rows,
        P(expert, None, cuts),
        P(expert, None, cuts),
        P(expert, cuts, None),
        P(expert, None, cuts),
        P(expert, None, cuts),
    )
    return jax.shard_map(shards, mesh=fine, in_specs=in_specs, out_specs=rows, check_vma=False)
```

```python
import jax
import jax.numpy as jnp
from jax import lax
from jax.sharding import Mesh, PartitionSpec as P

BF = jnp.bfloat16
F32 = jnp.float32
SLAB = ("core", "y", "x")
SIDE = 4


def hop(value, order, step, leave=False, join=False):
    pairs = []
    for core in range(2):
        axis_core = 1 - core if join else core
        to_core = 1 - core if leave or join else core
        for y in range(SIDE):
            for x in range(SIDE):
                to_y, to_x = y, x
                if axis_core == order:
                    to_x = (x + step) % SIDE
                else:
                    to_y = (y + step) % SIDE
                pairs.append(((core * SIDE + y) * SIDE + x, (to_core * SIDE + to_y) * SIDE + to_x))
    return lax.ppermute(value, SLAB, pairs)


def swap(value):
    return lax.ppermute(value, "core", [(0, 1), (1, 0)])


def rank_slots(flat_routes):
    count = flat_routes.shape[0]
    positions = jnp.arange(count, dtype=jnp.int32)
    before = positions[:, None] < positions[None, :]
    matches = flat_routes[:, None] == flat_routes[None, :]
    return jnp.sum(jnp.logical_and(matches, before), axis=0)


def exact(choice, value):
    return jnp.dot(choice.astype(BF), value, preferred_element_type=F32)


def expert_rows(grad_rows, gate_mat, up_mat, down_mat, pre_gate, pre_up):
    contract = (((1,), (1,)), ((), ()))
    hidden_grad = lax.dot_general(grad_rows, down_mat, contract, preferred_element_type=F32)
    gate_vals = pre_gate.astype(F32)
    up_vals = pre_up.astype(F32)
    sigmoid_gate = jax.nn.sigmoid(gate_vals)
    up_grad = (hidden_grad * gate_vals * sigmoid_gate).astype(BF)
    gate_grad = (
        hidden_grad * up_vals * sigmoid_gate * (1.0 + gate_vals * (1.0 - sigmoid_gate))
    ).astype(BF)
    partial_value = lax.dot_general(gate_grad, gate_mat, contract, preferred_element_type=F32)
    partial_value += lax.dot_general(up_grad, up_mat, contract, preferred_element_type=F32)
    return partial_value.astype(BF)


def add(*values):
    return sum(v.astype(F32) for v in values)


def shards(out_grad, routes, gate_weight, gate_proj, up_proj, down_proj, saved_gate, saved_up):
    tok, dim = out_grad.shape
    my_x, my_y = lax.axis_index("x"), lax.axis_index("y")
    core = lax.axis_index("core")

    flat_routes = routes.reshape(-1)
    slot = rank_slots(flat_routes)
    key = ((flat_routes // 2) * 2 + (flat_routes + core) % 2) * 4 + slot
    key = key.reshape(tok, 2)
    places = jnp.arange(32, dtype=jnp.int32)
    far_z = ((places // 8 + lax.axis_index("zh")) % 4) * 2 + (places // 4) % 2
    match = (far_z * 4 + places % 4)[:, None, None] == key[None, :, :]
    weight = jnp.sum(jnp.where(match, gate_weight[None], 0.0), axis=(1, 2))
    chosen = jnp.any(match, axis=2)
    outgoing = (exact(chosen, out_grad) * weight[:, None]).astype(BF)
    arrived = [outgoing[:8]] + [
        lax.ppermute(outgoing[8 * k:8 * k + 8], "zh", [(i, (i + k) % 4) for i in range(4)])
        for k in (1, 2, 3)
    ]
    arrived = jnp.concatenate(arrived, 0)
    pair = [(0, 1), (1, 0)]
    turned = (places % 16) // 4 * 8 + places // 16 * 4 + places % 4
    turn = turned[:, None] == places[None, :]
    own = exact(turn, arrived).astype(BF)
    layers = (own, lax.ppermute(own, "zl", pair))
    rings = [(v, hop(v, 0, 1), hop(v, 0, -1), hop(v, 0, 2)) for v in layers]
    line = [
        jnp.concatenate([v[k * 16:k * 16 + 16] for pieces in zip(*rings) for v in pieces], 0)
        for k in (0, 1)
    ]
    line, saved_gate, saved_up = lax.optimization_barrier((line, saved_gate, saved_up))

    def saved_rows(*parts):
        i = jnp.arange(128 * len(parts), dtype=jnp.int32)
        outer = jnp.asarray([p[0] for p in parts], jnp.int32)[i // 128]
        source = (core + jnp.asarray([p[1] for p in parts], jnp.int32)[i // 128]) % 2
        inner = jnp.asarray((0, 3, 1, 2), jnp.int32)[(i // 32) % 4]
        step_y = jnp.where(source == 0, outer, inner)
        step_x = jnp.where(source == 0, inner, outer)
        low = (lax.axis_index("zl") + (i // 16) % 2) % 2
        high = (lax.axis_index("zh") + 4 - (i // 4) % 4) % 4
        block = ((my_y + step_y) % 4 * 2 + low) * 4 + (my_x + step_x) % 4
        row = block * 32 + (high * 2 + source) * 4 + i % 4
        choice = row[:, None] == jnp.arange(saved_gate.shape[1], dtype=jnp.int32)[None, :]
        return exact(choice, saved_gate[0]).astype(BF), exact(choice, saved_up[0]).astype(BF)

    pre_line, pre_early, pre_late, pre_end = (
        saved_rows((0, 0), (0, 1)),
        saved_rows((3, 0), (1, 1)),
        saved_rows((1, 0), (3, 1)),
        saved_rows((2, 0), (2, 1)),
    )
    pre_line, pre_early, pre_late, pre_end = lax.optimization_barrier(
        (pre_line, pre_early, pre_late, pre_end)
    )
    weights = (gate_proj[0], up_proj[0], down_proj[0])

    def work(mine, others, saved):
        result = expert_rows(jnp.concatenate([mine, others], 0), *weights, *saved)
        return result[:128], result[128:]

    line_other = swap(line[1])
    back0, ahead1 = hop(line[0], 1, 1), hop(line[1], 1, -1)
    line, line_other = lax.optimization_barrier((line, line_other))
    back_other, ahead0 = hop(line[1], 1, 1, leave=True), hop(line[0], 1, -1)
    end0, end1 = hop(back0, 1, 1), hop(ahead1, 1, -1, leave=True)
    ahead_other = swap(ahead1)
    middle = work(line[0], line_other, pre_line)
    middle, ahead_other = lax.optimization_barrier((middle, ahead_other))
    early = work(back0, ahead_other, pre_early)
    early, ahead0, back_other = lax.optimization_barrier((early, ahead0, back_other))
    got_ahead0, got_back1 = hop(early[0], 1, -1), hop(early[1], 1, 1, join=True)
    late = work(ahead0, back_other, pre_late)
    middle_other = swap(middle[1])
    late, end0, end1, middle_other = lax.optimization_barrier((late, end0, end1, middle_other))
    ends = work(end0, end1, pre_end)
    far0, far1 = hop(ends[0], 1, 1), hop(ends[1], 1, -1, join=True)
    late_other = swap(late[1])
    far0, far1, got_ahead0, got_back1, late_other = lax.optimization_barrier(
        (far0, far1, got_ahead0, got_back1, late_other)
    )
    got_back0 = hop(add(late[0], far0).astype(BF), 1, 1)
    got_ahead1 = hop(add(late_other, far1).astype(BF), 1, -1)
    sums = [add(middle[0], got_back0, got_ahead0), add(middle_other, got_back1, got_ahead1)]
    mine, to_before, to_after, to_far = [
        jnp.concatenate([s[k * 32:k * 32 + 32] for s in sums], 0) for k in range(4)
    ]
    got_far = hop(to_far.astype(BF), 0, 2)
    got_before = hop(to_after.astype(BF), 0, 1)
    got_after = hop(to_before.astype(BF), 0, -1)
    total = add(mine, got_before, got_after, got_far)
    places = jnp.arange(64, dtype=jnp.int32)
    away = (places // 8 + lax.axis_index("zl")) % 2
    steps = (lax.axis_index("zh") + 4 - places // 16) % 4
    home = (places // 4 % 2) * 32 + away * 16 + steps * 4 + places % 4
    total = exact(home[:, None] == places[None, :], total.astype(BF)).astype(BF)
    returned = lax.all_to_all(total, ("zh", "zl"), split_axis=0, concat_axis=0, tiled=True)
    row_key = ((places // 16) * 2 + places // 4 % 2) * 4 + places % 4
    picked = jnp.any(row_key[None, :, None] == key[:, None, :], axis=2)
    return exact(picked, returned).astype(BF)


def solution(mesh):
    fine = Mesh(mesh.devices.reshape(4, 2, 4, 2, 4), ("zh", "core", "y", "zl", "x"))
    expert, cuts = ("zh", "core"), ("y", "zl", "x")
    rows = P(expert + cuts, None)
    in_specs = (
        rows,
        rows,
        rows,
        P(expert, None, cuts),
        P(expert, None, cuts),
        P(expert, cuts, None),
        P(expert, None, cuts),
        P(expert, None, cuts),
    )
    return jax.shard_map(shards, mesh=fine, in_specs=in_specs, out_specs=rows, check_vma=False)
```

```python
import jax
import jax.numpy as jnp
from jax import lax
from jax.sharding import Mesh, PartitionSpec as P

BF = jnp.bfloat16
F32 = jnp.float32
SLAB = ("core", "y", "x")
SIDE = 4


def hop(value, order, step, leave=False, join=False):
    pairs = []
    for core in range(2):
        axis_core = 1 - core if join else core
        to_core = 1 - core if leave or join else core
        for y in range(SIDE):
            for x in range(SIDE):
                to_y, to_x = y, x
                if axis_core == order:
                    to_x = (x + step) % SIDE
                else:
                    to_y = (y + step) % SIDE
                pairs.append(((core * SIDE + y) * SIDE + x, (to_core * SIDE + to_y) * SIDE + to_x))
    return lax.ppermute(value, SLAB, pairs)


def swap(value):
    return lax.ppermute(value, "core", [(0, 1), (1, 0)])


def rank_slots(flat_routes):
    count = flat_routes.shape[0]
    positions = jnp.arange(count, dtype=jnp.int32)
    before = positions[:, None] < positions[None, :]
    matches = flat_routes[:, None] == flat_routes[None, :]
    return jnp.sum(jnp.logical_and(matches, before), axis=0)


def exact(choice, value):
    return jnp.dot(choice.astype(BF), value, preferred_element_type=F32)


def expert_rows(grad_rows, gate_mat, up_mat, down_mat, pre_gate, pre_up):
    contract = (((1,), (1,)), ((), ()))
    hidden_grad = lax.dot_general(grad_rows, down_mat, contract, preferred_element_type=F32)
    gate_vals = pre_gate.astype(F32)
    up_vals = pre_up.astype(F32)
    sigmoid_gate = jax.nn.sigmoid(gate_vals)
    up_grad = (hidden_grad * gate_vals * sigmoid_gate).astype(BF)
    gate_grad = (
        hidden_grad * up_vals * sigmoid_gate * (1.0 + gate_vals * (1.0 - sigmoid_gate))
    ).astype(BF)
    partial_value = lax.dot_general(gate_grad, gate_mat, contract, preferred_element_type=F32)
    partial_value += lax.dot_general(up_grad, up_mat, contract, preferred_element_type=F32)
    return partial_value.astype(BF)


def add(*values):
    return sum(v.astype(F32) for v in values)


def shards(out_grad, routes, gate_weight, gate_proj, up_proj, down_proj, saved_gate, saved_up):
    tok, dim = out_grad.shape
    my_x, my_y = lax.axis_index("x"), lax.axis_index("y")
    core = lax.axis_index("core")

    flat_routes = routes.reshape(-1)
    slot = rank_slots(flat_routes)
    key = ((flat_routes // 2) * 2 + (flat_routes + core) % 2) * 4 + slot
    key = key.reshape(tok, 2)
    places = jnp.arange(32, dtype=jnp.int32)
    far_z = ((places // 8 + lax.axis_index("zh")) % 4) * 2 + (places // 4) % 2
    match = (far_z * 4 + places % 4)[:, None, None] == key[None, :, :]
    weight = jnp.sum(jnp.where(match, gate_weight[None], 0.0), axis=(1, 2))
    chosen = jnp.any(match, axis=2)
    outgoing = (exact(chosen, out_grad) * weight[:, None]).astype(BF)
    arrived = [outgoing[:8]] + [
        lax.ppermute(outgoing[8 * k:8 * k + 8], "zh", [(i, (i + k) % 4) for i in range(4)])
        for k in (1, 2, 3)
    ]
    arrived = jnp.concatenate(arrived, 0)
    pair = [(0, 1), (1, 0)]
    turned = (places % 16) // 4 * 8 + places // 16 * 4 + places % 4
    turn = turned[:, None] == places[None, :]
    own = exact(turn, arrived).astype(BF)
    layers = (own, lax.ppermute(own, "zl", pair))
    rings = [(v, hop(v, 0, 1), hop(v, 0, -1), hop(v, 0, 2)) for v in layers]
    line = [
        jnp.concatenate([v[k * 16:k * 16 + 16] for pieces in zip(*rings) for v in pieces], 0)
        for k in (0, 1)
    ]
    line_other = swap(line[1])
    back0, ahead1 = hop(line[0], 1, 1), hop(line[1], 1, -1)
    line, line_other, saved_gate, saved_up = lax.optimization_barrier(
        (line, line_other, saved_gate, saved_up)
    )

    def saved_rows(*parts):
        i = jnp.arange(128 * len(parts), dtype=jnp.int32)
        outer = jnp.asarray([p[0] for p in parts], jnp.int32)[i // 128]
        source = (core + jnp.asarray([p[1] for p in parts], jnp.int32)[i // 128]) % 2
        inner = jnp.asarray((0, 3, 1, 2), jnp.int32)[(i // 32) % 4]
        step_y = jnp.where(source == 0, outer, inner)
        step_x = jnp.where(source == 0, inner, outer)
        low = (lax.axis_index("zl") + (i // 16) % 2) % 2
        high = (lax.axis_index("zh") + 4 - (i // 4) % 4) % 4
        block = ((my_y + step_y) % 4 * 2 + low) * 4 + (my_x + step_x) % 4
        row = block * 32 + (high * 2 + source) * 4 + i % 4
        choice = row[:, None] == jnp.arange(saved_gate.shape[1], dtype=jnp.int32)[None, :]
        return exact(choice, saved_gate[0]).astype(BF), exact(choice, saved_up[0]).astype(BF)

    pre_line, pre_early, pre_late, pre_end = (
        saved_rows((0, 0), (0, 1)),
        saved_rows((3, 0), (1, 1)),
        saved_rows((1, 0), (3, 1)),
        saved_rows((2, 0), (2, 1)),
    )
    pre_line, pre_early, pre_late, pre_end = lax.optimization_barrier(
        (pre_line, pre_early, pre_late, pre_end)
    )
    weights = (gate_proj[0], up_proj[0], down_proj[0])

    def work(mine, others, saved):
        result = expert_rows(jnp.concatenate([mine, others], 0), *weights, *saved)
        return result[:128], result[128:]

    back_other, ahead0 = hop(line[1], 1, 1, leave=True), hop(line[0], 1, -1)
    end0, end1 = hop(back0, 1, 1), hop(ahead1, 1, -1, leave=True)
    ahead_other = swap(ahead1)
    middle = work(line[0], line_other, pre_line)
    middle, ahead_other = lax.optimization_barrier((middle, ahead_other))
    early = work(back0, ahead_other, pre_early)
    early, ahead0, back_other = lax.optimization_barrier((early, ahead0, back_other))
    got_ahead0, got_back1 = hop(early[0], 1, -1), hop(early[1], 1, 1, join=True)
    late = work(ahead0, back_other, pre_late)
    middle_other = swap(middle[1])
    late, end0, end1, middle_other = lax.optimization_barrier((late, end0, end1, middle_other))
    ends = work(end0, end1, pre_end)
    far0, far1 = hop(ends[0], 1, 1), hop(ends[1], 1, -1, join=True)
    late_other = swap(late[1])
    far0, far1, got_ahead0, got_back1, late_other = lax.optimization_barrier(
        (far0, far1, got_ahead0, got_back1, late_other)
    )
    got_back0 = hop(add(late[0], far0).astype(BF), 1, 1)
    got_ahead1 = hop(add(late_other, far1).astype(BF), 1, -1)
    sums = [add(middle[0], got_back0, got_ahead0), add(middle_other, got_back1, got_ahead1)]
    mine, to_before, to_after, to_far = [
        jnp.concatenate([s[k * 32:k * 32 + 32] for s in sums], 0) for k in range(4)
    ]
    got_far = hop(to_far.astype(BF), 0, 2)
    got_before = hop(to_after.astype(BF), 0, 1)
    got_after = hop(to_before.astype(BF), 0, -1)
    total = add(mine, got_before, got_after, got_far)
    places = jnp.arange(64, dtype=jnp.int32)
    away = (places // 8 + lax.axis_index("zl")) % 2
    steps = (lax.axis_index("zh") + 4 - places // 16) % 4
    home = (places // 4 % 2) * 32 + away * 16 + steps * 4 + places % 4
    total = exact(home[:, None] == places[None, :], total.astype(BF)).astype(BF)
    returned = lax.all_to_all(total, ("zh", "zl"), split_axis=0, concat_axis=0, tiled=True)
    row_key = ((places // 16) * 2 + places // 4 % 2) * 4 + places % 4
    picked = jnp.any(row_key[None, :, None] == key[:, None, :], axis=2)
    return exact(picked, returned).astype(BF)


def solution(mesh):
    fine = Mesh(mesh.devices.reshape(4, 2, 4, 2, 4), ("zh", "core", "y", "zl", "x"))
    expert, cuts = ("zh", "core"), ("y", "zl", "x")
    rows = P(expert + cuts, None)
    in_specs = (
        rows,
        rows,
        rows,
        P(expert, None, cuts),
        P(expert, None, cuts),
        P(expert, cuts, None),
        P(expert, None, cuts),
        P(expert, None, cuts),
    )
    return jax.shard_map(shards, mesh=fine, in_specs=in_specs, out_specs=rows, check_vma=False)
```
